32 devices in a mesh: rows: 8 (over z, y), serve: 4 (over x, core).
Axes of the slice: x: 2, y: 2, z: 4, core: 2. Of those that a mesh axis runs over, the one named last changes fastest.
Arguments:
- rows_small: float32 [32768, 32], P(('rows', 'serve')), may hold values from -6 to 6
- rows_mid: float32 [32768, 64], P(('rows', 'serve')), may hold values from -6 to 6
- rows_wide: float32 [32768, 128], P(('rows', 'serve')), may hold values from -6 to 6
- row_grads: float32 [3, 32768, 256], P(None, ('rows', 'serve'))
- proj_small: float32 [32, 256], replicated, may hold values from -1 to 1
- proj_mid: float32 [64, 256], replicated, may hold values from -0.75 to 0.75
- proj_wide: float32 [128, 256], replicated, may hold values from -0.5 to 0.5
- counts: int32 [3, 32], P(None, ('rows', 'serve')), may hold values from 512 to 1024, as said below
- owners: int32 [3, 32768, 1], P(None, ('rows', 'serve')), may hold values from 0 to 31; in each aligned block of 1024 rows (0 to 1023, 1024 to 2047, ..., all dimensions but the last counted through in order) at most 48 rows name the same one
Outputs:
- served: bfloat16 [49152, 768], P(('rows', 'serve'))
The draws below stay inside these ranges and needn't reach their ends.
Inputs may be any that keep to these rules, and one draw needn't show every extreme that they name: `counts`: one device of each tier has all 1024 slots live. `owners`: among the 1024 slots of one device and tier at most 48 name one owner, and exactly 48 do for some owner.
All inputs are finite; a program needn't handle non-finite values.
Results may differ from the reference program's by a relative error of at most 0.001.
Values may be sent and summed in bfloat16 or wider, within the bound.
No kernel may reach another device: no remote copies, remote signals or barrier semaphores. Data moves between devices by JAX's collectives and lax.ppermute only.
A program may use at most 64 MiB of HBM per device.

```python
import math
import jax
import jax.numpy as jnp
import numpy as np
from jax import lax

W_SMALL = 32
W_MID = 64
W_WIDE = 128
D_OUT = 256
ROWS_DEV = 1024
ALL_DEVS = 32
TOTAL_ROWS = 32768
CAP = 48
N_ROWS = 8
N_SERVE = 4


def draw_row_grads(key, part):
    key = jax.random.fold_in(key, 11)
    first_key = jax.random.fold_in(key, 0)
    device_of = (jnp.arange(TOTAL_ROWS) // ROWS_DEV).astype(jnp.float32)
    rising = 1.0 + 2.0 * device_of / max(ALL_DEVS - 1, 1)
    values = jax.random.normal(first_key, (3, TOTAL_ROWS, D_OUT)) * rising[None, :, None]
    return values.astype(jnp.float32)


def draw_counts(key, part):
    key = jax.random.fold_in(key, 5)
    first_key, second_key = jax.random.split(key, 2)
    cuts = jax.random.randint(first_key, (3, ALL_DEVS), 0, ROWS_DEV // 256 + 1)
    chosen = jax.random.randint(second_key, (3, 1), 0, ALL_DEVS)
    cuts = jnp.where(jnp.arange(ALL_DEVS)[None, :] == chosen, 0, cuts)
    return (ROWS_DEV - 128 * cuts).astype(jnp.int32)


def steps_of(own_key, extent, cuts, low, high):
    factor_of = 1.0
    for dim, parts in cuts:
        draws = jax.random.uniform(jax.random.fold_in(jax.random.fold_in(own_key, 6), dim), (parts,), jnp.float32, low / len(cuts), high / len(cuts))
        factor_of = factor_of * jnp.repeat(jnp.exp(draws), extent[dim] // parts).reshape((-1,) + (1,) * (len(extent) - 1 - dim))
    return factor_of


def deal_out(key, own, number, rows, number_of, top, bound, lean):
    order = jax.random.permutation(key, number_of)
    crowded, usual = portions_of(number_of, rows * top, bound, lean, True), portions_of(number_of, rows * top, bound, lean, False)
    places = jnp.arange(number_of)

    def named(sizes, rotation):
        used = int((sizes > 0).sum())
        fixed = max(1, used // 4)
        moved = fixed + (places - fixed + rotation * (used - fixed)) % max(1, number_of - fixed)
        return jnp.zeros((number_of,), jnp.int32).at[order[jnp.where(places < fixed, places, moved)]].set(jnp.asarray(sizes, jnp.int32))

    sizes = jnp.where(number % 4 == 0, named(crowded, number // 4), named(usual, number - number // 4 - 1))
    mixed = jax.random.permutation(jax.random.fold_in(own, 3), number_of)
    donor, receiver = mixed[0:number_of // 2 * 2:2], mixed[1:number_of // 2 * 2:2]
    margin = jnp.minimum(sizes[donor] - 1, bound - sizes[receiver]) // 2
    margin = jnp.where((donor == order[0]) | (receiver == order[0]) | (sizes[receiver] == 0), 0, jnp.maximum(margin, 0))
    moved = jax.random.randint(jax.random.fold_in(own, 4), (number_of // 2,), 0, 1 << 20) % (margin + 1)
    sizes = sizes.at[donor].add(-moved).at[receiver].add(moved)
    members = jnp.searchsorted(jnp.cumsum(sizes), jnp.arange(rows * top), side="right").astype(jnp.int32)
    table = members.reshape(top, rows).T
    table = table[jax.random.permutation(jax.random.fold_in(own, 1), rows)]
    rotation = jax.random.randint(jax.random.fold_in(own, 2), (rows, 1), 0, top)
    return jnp.take_along_axis(table, (jnp.arange(top)[None, :] + rotation) % top, axis=1)


def portions_of(count, total, limit, lean, full):
    loads = [(1 << 20) // math.isqrt(rank ** lean) + 1 for rank in range(1, count + 1)]
    largest = limit if full else min(limit, max(-(-total // count), total * loads[0] // sum(loads)))
    least = 1 if total - largest >= count - 1 else 0
    holding, spare = [largest] + [least] * (count - 1), total - largest - least * (count - 1)
    while spare > 0:
        free = [i for i in range(1, count) if holding[i] < largest] or [i for i in range(1, count) if holding[i] < limit]
        whole, budget = sum([loads[i] for i in free]), spare
        for i in free:
            more = min(limit - holding[i], max(1, budget * loads[i] // whole), spare)
            holding[i] = holding[i] + more
            spare = spare - more
    return np.array(holding)


def gaussian(own_key, shape, width, reach, cuts=(), held_as=jnp.bfloat16):
    level = steps_of(own_key, shape, cuts, -0.22, 0.18) if cuts else 1.0
    array = jax.random.normal(own_key, shape, jnp.float32) * width * level
    return jnp.minimum(jnp.maximum(array, -reach), reach).astype(held_as)


def setup_inputs(seed: int = 0) -> dict:
    keys = jax.random.split(jax.random.key(seed), 10)
    rows_small = gaussian(keys[0], (TOTAL_ROWS, W_SMALL), 1.0, 6.0, ((0, 32),), jnp.float32)
    rows_mid = gaussian(keys[1], (TOTAL_ROWS, W_MID), 1.0, 6.0, ((0, 32),), jnp.float32)
    rows_wide = gaussian(keys[2], (TOTAL_ROWS, W_WIDE), 1.0, 6.0, ((0, 32),), jnp.float32)
    row_grads = draw_row_grads(jax.random.fold_in(keys[9], 71), 0)
    proj_small = gaussian(keys[4], (W_SMALL, D_OUT), W_SMALL ** -0.5, 1.0, (), jnp.float32)
    proj_mid = gaussian(keys[5], (W_MID, D_OUT), W_MID ** -0.5, 0.75, (), jnp.float32)
    proj_wide = gaussian(keys[6], (W_WIDE, D_OUT), W_WIDE ** -0.5, 0.5, (), jnp.float32)
    counts = draw_counts(jax.random.fold_in(keys[9], 71), 0)
    owners_keys = jax.random.split(jax.random.fold_in(keys[8], 1), 3 * TOTAL_ROWS // ROWS_DEV)
    owners_turns = jax.random.permutation(jax.random.fold_in(keys[8], 3), 3 * TOTAL_ROWS // ROWS_DEV)
    owners = jax.vmap(lambda own, number: deal_out(jax.random.fold_in(keys[8], 2), own, number, ROWS_DEV, ALL_DEVS, 1, CAP, 2))(owners_keys, owners_turns).reshape((3, TOTAL_ROWS, 1))
    return dict(rows_small=rows_small, rows_mid=rows_mid, rows_wide=rows_wide, row_grads=row_grads, proj_small=proj_small, proj_mid=proj_mid, proj_wide=proj_wide, counts=counts, owners=owners)


STEP_NORM = 16.0
ROW_RATE = 0.1

def refresh(projection, total):
    factor = STEP_NORM / jnp.sqrt(jnp.sum(total * total) + 1e-06)
    return projection - factor * total

def reference(rows_small, rows_mid, rows_wide, row_grads, proj_small, proj_mid, proj_wide, counts, owners):
    device_count = N_ROWS * N_SERVE
    capacity = CAP
    tables = (rows_small, rows_mid, rows_wide)
    projections = (proj_small, proj_mid, proj_wide)
    positions = jnp.arange(ROWS_DEV, dtype=jnp.int32)
    sources = jnp.arange(TOTAL_ROWS, dtype=jnp.int32) // ROWS_DEV
    columns = jnp.arange(device_count, dtype=jnp.int32)
    outside = device_count * device_count * capacity
    served = jnp.zeros((outside, 3 * D_OUT), jnp.bfloat16)
    for tier_index in range(3):
        table = tables[tier_index]
        projection = projections[tier_index]
        valid = (positions[None, :] < counts[tier_index][:, None]).reshape(-1)
        gradients = jnp.where(valid[:, None], row_grads[tier_index], 0.0)
        total = jnp.dot(table.T, gradients, precision=lax.Precision.HIGHEST, preferred_element_type=jnp.float32)
        new_proj = refresh(projection, total)
        row_step = jnp.dot(gradients, projection.T, precision=lax.Precision.HIGHEST, preferred_element_type=jnp.float32)
        new_rows = table - ROW_RATE * row_step
        projected = jnp.dot(new_rows, new_proj, precision=lax.Precision.HIGHEST, preferred_element_type=jnp.float32).astype(jnp.bfloat16)
        owner = owners[tier_index, :, 0]
        matched = (owner[:, None] == columns[None, :]) & valid[:, None]
        hit_counts = matched.astype(jnp.int32).reshape(device_count, ROWS_DEV, device_count)
        before = (jnp.cumsum(hit_counts, axis=1) - hit_counts).reshape(TOTAL_ROWS, device_count)
        slot_index = lax.optimization_barrier(jnp.sum(jnp.where(matched, before, 0), axis=1)).astype(jnp.int32)
        target = owner * (device_count * capacity) + sources * capacity + slot_index
        target = jnp.where(valid, target, outside).astype(jnp.int32)
        served = served.at[target, tier_index * D_OUT:(tier_index + 1) * D_OUT].set(projected, mode='drop')
    return served
```

```python
import functools

import jax
import jax.numpy as jnp
from jax import lax
from jax.experimental import pallas as pl
from jax.experimental.pallas import tpu as pltpu
from jax.sharding import PartitionSpec as P

STEP_NORM = 16.0
ROW_RATE = 0.1
LANES = 128
CHUNK = 8
CODE_BITS = 14.9999
CODE_STEPS = 8.0
MIB = 1024 * 1024


def halves(value):
    high = value.astype(jnp.bfloat16)
    low = (value - high.astype(jnp.float32)).astype(jnp.bfloat16)
    return high, low


def contract(left, right, left_dim, right_dim):
    return lax.dot_general(
        left,
        right,
        (((left_dim,), (right_dim,)), ((), ())),
        preferred_element_type=jnp.float32,
    )


def row_top(values):
    return jnp.max(values, axis=1, keepdims=True)


def code_exponent(largest):
    return jnp.ceil(CODE_STEPS * jnp.log2(jnp.maximum(largest, 1e-30)))


def code(value, exponent):
    scaled = value * jnp.exp2(CODE_BITS - exponent * (1.0 / CODE_STEPS))
    return jnp.clip(jnp.floor(scaled + 0.5), -32767.0, 32767.0)


def code_scale(exponent):
    return jnp.exp2(exponent * (1.0 / CODE_STEPS) - CODE_BITS)


def whole(shape):
    return pl.BlockSpec(shape, lambda step: (0,) * len(shape))


def start_copies(sources, held, done):
    copies = [
        pltpu.make_async_copy(source, target, done.at[index])
        for index, (source, target) in enumerate(zip(sources, held))
    ]
    for copy in copies:
        copy.start()
    return copies


def share_codes(value):
    exponent = code_exponent(jnp.broadcast_to(row_top(jnp.abs(value)), value.shape))
    scaled = value * jnp.exp2(CODE_BITS + 8.0 - exponent * (1.0 / CODE_STEPS))
    whole_code = jnp.clip(jnp.floor(scaled + 0.5), -8388352.0, 8388352.0)
    upper = jnp.floor(whole_code * (1.0 / 256.0))
    lower = whole_code - 256.0 * upper
    upper = jnp.where(share_row(value.shape), exponent_row(exponent), upper)
    lower = lower[:, :LANES] * 256.0 + lower[:, LANES:] - 32768.0
    return jnp.concatenate([upper[:, :LANES], upper[:, LANES:], lower], axis=0)


def share_values(coded):
    upper = jnp.concatenate([coded[:CHUNK], coded[CHUNK : 2 * CHUNK]], axis=1)
    lower = coded[2 * CHUNK :] + 32768.0
    first = jnp.floor(lower * (1.0 / 256.0))
    lower = jnp.concatenate([first, lower - 256.0 * first], axis=1)
    scale = code_scale(exponent_column(upper)) * (1.0 / 256.0)
    return (upper * 256.0 + lower) * scale


def share_row(shape):
    return lax.broadcasted_iota(jnp.int32, shape, 0) == CHUNK - 1


def exponent_row(exponent):
    row = lax.broadcasted_iota(jnp.int32, exponent.shape, 0)
    lane = lax.broadcasted_iota(jnp.int32, exponent.shape, 1)
    return jnp.sum(jnp.where(row == lane, exponent, 0.0), axis=0, keepdims=True)


def exponent_column(coded):
    row = lax.broadcasted_iota(jnp.int32, coded.shape, 0)
    lane = lax.broadcasted_iota(jnp.int32, coded.shape, 1)
    exponents = jnp.where(row == lane, coded[CHUNK - 1 :], 0.0)
    return jnp.sum(exponents, axis=1, keepdims=True)


def owner_ranks(owner, live_count, device_count):
    slots = owner.shape[1]
    live = lax.broadcasted_iota(jnp.int32, (1, slots), 1) < live_count
    owner = jnp.where(live, owner, -1)
    named = lax.broadcasted_iota(jnp.int32, (device_count, slots), 0) == owner
    matched = jnp.where(named, 1.0, 0.0)
    parts = [matched[:, at : at + LANES] for at in range(0, slots, LANES)]
    stacked = jnp.concatenate(parts, axis=0).astype(jnp.bfloat16)
    row = lax.broadcasted_iota(jnp.int32, (LANES, 2 * LANES), 0)
    column = lax.broadcasted_iota(jnp.int32, (LANES, 2 * LANES), 1)
    counting = jnp.where((row < column) | (column >= LANES), 1.0, 0.0)
    sums = contract(stacked, counting.astype(jnp.bfloat16), 1, 0)
    running = jnp.zeros((device_count, LANES), jnp.float32)
    ranks = []
    for index, part in enumerate(parts):
        here = sums[index * device_count : (index + 1) * device_count]
        before = here[:, :LANES] + running
        ranks.append(jnp.sum(part * before, axis=0, keepdims=True))
        running = running + here[:, LANES:]
    return matched, jnp.concatenate(ranks, axis=1)


def rank_rows(rank, first, count):
    place = lax.broadcasted_iota(jnp.int32, (count, rank.shape[1]), 0) + first
    return jnp.where(place.astype(jnp.float32) == rank, 1.0, 0.0)


def moved_rows(table, projection, gradients):
    high, low = halves(projection)
    right = jnp.concatenate([high, low], axis=0)
    grad_high, grad_low = halves(gradients)
    product = contract(grad_high, right, 1, 1) + contract(grad_low, right, 1, 1)
    row_step = product[:, :LANES] + product[:, LANES:]
    return halves(table - ROW_RATE * row_step)


def in_lanes(pair, first, count):
    lane = lax.broadcasted_iota(jnp.int32, pair[0].shape, 1)
    kept = (lane >= first) & (lane < first + count)
    pair = [jnp.where(kept, half.astype(jnp.float32), 0.0) for half in pair]
    return jnp.concatenate(pair, axis=1).astype(jnp.bfloat16)


def widened(value, first):
    count, columns = value.shape
    above = [jnp.zeros((first, columns), value.dtype)] if first else []
    below = LANES - first - count
    below = [jnp.zeros((below, columns), value.dtype)] if below else []
    return jnp.concatenate(above + [value] + below, axis=0)


def packing(padded):
    share = 2 * CHUNK
    mid = share + padded // 2
    return share, mid, mid + padded // 3


def repeated(value, times):
    rest = LANES - times * value.shape[0]
    below = [jnp.zeros((rest, value.shape[1]), value.dtype)] if rest else []
    return jnp.concatenate([value] * times + below, axis=0)


def spread(column, rows):
    return jnp.broadcast_to(column, (rows, LANES))


def first_kernel(device_count, padded, group, counts, *refs):
    count = 8
    sources, out, held = refs[:count], refs[count], refs[count + 1 : 2 * count + 1]
    stacked, placed, ready, done, sent = refs[2 * count + 1 :]
    copies = start_copies(sources, held, done)
    owners, small, grads_small, mid, grads_mid, wide, proj_wide, grads_wide = held
    slots = wide.shape[0]
    w_small, w_mid, w_wide = small.shape[0], mid.shape[0], wide.shape[1]
    filled = w_wide + w_mid + w_small
    third = padded // 3

    def gradient_halves(grads):
        high, low = halves(grads[...])
        return jnp.concatenate([high, low], axis=1)

    def folded(product, width):
        out_width = product.shape[1] // 2
        upper = product[:width, :out_width] + product[:width, out_width:]
        return upper + (product[width:, :out_width] + product[width:, out_width:])

    def from_columns(table, grads, tier):
        width = table.shape[0]
        live = lax.broadcasted_iota(jnp.int32, (width, slots), 1) < counts[0, tier]
        high, low = halves(jnp.where(live, table[...], 0.0))
        left = jnp.concatenate([high, low], axis=0)
        return folded(contract(left, gradient_halves(grads), 1, 0), width)

    stacked[filled:, :] = jnp.zeros(
        (stacked.shape[0] - filled, stacked.shape[1]), jnp.float32
    )
    copies[0].wait()
    matched, rank = owner_ranks(owners[0], counts[0, 2], device_count)
    ranks = rank_rows(rank, 0, padded).astype(jnp.bfloat16)
    for copy in copies[1:3]:
        copy.wait()
    stacked[w_wide + w_mid : filled, :] = from_columns(small, grads_small, 0)
    for copy in copies[3:5]:
        copy.wait()
    stacked[w_wide : w_wide + w_mid, :] = from_columns(mid, grads_mid, 1)
    for copy in copies[5:8]:
        copy.wait()
    live = lax.broadcasted_iota(jnp.int32, (slots, w_wide), 0) < counts[0, 2]
    high, low = halves(jnp.where(live, wide[...], 0.0))
    left = jnp.concatenate([high, low], axis=1)
    product = contract(left, gradient_halves(grads_wide), 0, 0)
    stacked[0:w_wide, :] = folded(product, w_wide)
    moved = moved_rows(wide[...], proj_wide[...], grads_wide[...])
    placed[...] = jnp.concatenate(moved, axis=1)

    row = lax.broadcasted_iota(jnp.int32, (padded, LANES), 0) + CHUNK
    lane = lax.broadcasted_iota(jnp.int32, (padded, LANES), 1)
    diagonal = row == lane
    leaving = []
    for first in range(0, device_count, group):
        chosen = []
        for device in range(first, first + group):
            named = jnp.broadcast_to(matched[device : device + 1], (third, slots))
            named = named.astype(jnp.bfloat16)
            for at in range(3):
                chosen.append(ranks[at * third : (at + 1) * third] * named)
        pair = contract(jnp.concatenate(chosen, axis=0), placed[...], 1, 0)
        values = pair[:, :LANES] + pair[:, LANES:]
        top = spread(row_top(jnp.abs(values)), group * padded)
        exponent = code_exponent(top)
        coded = code(values, exponent).astype(jnp.int32)
        coded = coded.reshape(group, padded, LANES).astype(jnp.int16)
        ready[first : first + group, 0:padded, :] = coded
        exponent = exponent.reshape(group, padded, LANES)
        for device in range(first, first + group):
            start = device * (CHUNK - 1)
            share = share_codes(stacked[start : start + CHUNK])
            scales = jnp.where(diagonal, exponent[device - first], 0.0)
            scales = jnp.sum(scales, axis=0, keepdims=True)
            above = share[:CHUNK]
            spare = lax.broadcasted_iota(jnp.int32, above.shape, 1) >= CHUNK
            spare = spare & share_row(above.shape)
            share = jnp.concatenate(
                [jnp.where(spare, scales, above), share[CHUNK:]], axis=0
            )
            ready[device, padded:, :] = share.astype(jnp.int32).astype(jnp.int16)
        copy = pltpu.make_async_copy(
            ready.at[pl.ds(first, group)],
            out.at[pl.ds(first, group)],
            sent.at[first // group],
        )
        copy.start()
        leaving.append(copy)
    for copy in leaving:
        copy.wait()


def first_blocks(counts, small, mid, wide, grads, proj, owners, device_count, padded, group):
    slots, out_width = grads.shape[1:]
    block = (device_count, padded + 3 * CHUNK, LANES)

    def kernel(counts, owners, small, mid, wide, proj, grads, *rest):
        sources = (owners.at[pl.ds(2, 1)], small, grads.at[0], mid, grads.at[1])
        sources = sources + (wide, proj, grads.at[2])
        first_kernel(device_count, padded, group, counts, *sources, *rest)

    grad = pltpu.VMEM(grads.shape[1:], grads.dtype)
    held = [pltpu.VMEM((1,) + owners.shape[1:], owners.dtype)]
    held += [pltpu.VMEM(small.shape, small.dtype), grad]
    held += [pltpu.VMEM(mid.shape, mid.dtype), grad]
    held += [pltpu.VMEM(wide.shape, wide.dtype), pltpu.VMEM(proj.shape, proj.dtype), grad]
    return pl.pallas_call(
        kernel,
        out_shape=jax.ShapeDtypeStruct(block, jnp.int16),
        in_specs=[pl.BlockSpec(memory_space=pltpu.SMEM)]
        + [pl.BlockSpec(memory_space=pltpu.HBM)] * 6,
        out_specs=pl.BlockSpec(memory_space=pl.ANY),
        scratch_shapes=held
        + [
            pltpu.VMEM((device_count * CHUNK, out_width), jnp.float32),
            pltpu.VMEM((slots, 2 * LANES), jnp.bfloat16),
            pltpu.VMEM(block, jnp.int16),
            pltpu.SemaphoreType.DMA((8,)),
            pltpu.SemaphoreType.DMA((device_count // group,)),
        ],
        compiler_params=pltpu.CompilerParams(vmem_limit_bytes=56 * MIB),
        name="first_blocks",
    )(counts, owners, small, mid, wide, proj, grads)


def routing_kernel(device_count, padded, group, counts, *refs):
    count = 7
    sources, out, held = refs[:count], refs[count], refs[count + 1 : 2 * count + 1]
    placed, ready, done, sent = refs[2 * count + 1 :]
    copies = start_copies(sources, held, done)
    owners, small, proj_small, grads_small, mid, proj_mid, grads_mid = held
    w_small, w_mid = small.shape[0], mid.shape[0]
    slots = grads_mid.shape[0]
    half, third = padded // 2, padded // 3

    copies[0].wait()
    ranked = [
        owner_ranks(owners[tier], counts[0, tier], device_count) for tier in range(2)
    ]
    mid_ranks = [rank_rows(ranked[1][1], at * half, half) for at in range(2)]
    small_ranks = rank_rows(ranked[0][1], 0, padded).astype(jnp.bfloat16)
    for copy in copies[1:4]:
        copy.wait()
    table = repeated(small[...], 3).T
    moved = moved_rows(table, repeated(proj_small[...], 3), grads_small[...])
    for at in range(3):
        placed[2 + at] = in_lanes(moved, at * w_small, w_small)
    for copy in copies[4:7]:
        copy.wait()
    table = repeated(mid[...], 2).T
    moved = moved_rows(table, repeated(proj_mid[...], 2), grads_mid[...])
    for at in range(2):
        placed[at] = in_lanes(moved, at * w_mid, w_mid)

    def owner_row(tier, device, rows):
        return jnp.broadcast_to(ranked[tier][0][device : device + 1], (rows, slots))

    def picked(chosen, index):
        pair = contract(chosen, placed[index], 1, 0)
        return pair[:, :LANES] + pair[:, LANES:]

    spare = 3 * w_small
    leaving = []
    for first in range(0, device_count, group):
        devices = range(first, first + group)
        mid_rows = 0.0
        for at in range(2):
            chosen = [mid_ranks[at] * owner_row(1, device, half) for device in devices]
            chosen = jnp.concatenate(chosen, axis=0).astype(jnp.bfloat16)
            mid_rows = mid_rows + picked(chosen, at)
        named = [owner_row(0, device, third).astype(jnp.bfloat16) for device in devices]
        small_rows = 0.0
        for at in range(3):
            ranks = small_ranks[at * third : (at + 1) * third]
            chosen = jnp.concatenate([ranks * row for row in named], axis=0)
            small_rows = small_rows + picked(chosen, 2 + at)

        lane = lax.broadcasted_iota(jnp.int32, (group * half, LANES), 1)
        sizes = jnp.abs(mid_rows)
        mid_tops = [
            spread(row_top(jnp.where(side, sizes, 0.0)), group * half)
            for side in (lane < w_mid, lane >= w_mid)
        ]
        mid_top = jnp.where(lane < w_mid, mid_tops[0], mid_tops[1])
        lane = lax.broadcasted_iota(jnp.int32, (group * third, LANES), 1)
        sizes = jnp.abs(small_rows)
        by_slot = [top.reshape(group, half, LANES) for top in mid_tops]
        by_slot = jnp.concatenate(by_slot, axis=1)
        small_top = jnp.zeros((group * third, LANES), jnp.float32)
        for at in range(3):
            side = (lane >= at * w_small) & (lane < (at + 1) * w_small)
            top = row_top(jnp.where(side, sizes, 0.0))
            small_top = jnp.where(side | (lane == spare + at), top, small_top)
            top = by_slot[:, at * third : (at + 1) * third]
            top = top.reshape(group * third, LANES)
            small_top = jnp.where(lane == spare + 3 + at, top, small_top)

        small_exponent = code_exponent(small_top)
        small_code = code(small_rows, small_exponent)
        small_code = jnp.where(lane < spare, small_code, small_exponent)
        parts = (
            code(mid_rows, code_exponent(mid_top)).reshape(group, half, LANES),
            small_code.reshape(group, third, LANES),
        )
        coded = jnp.concatenate(parts, axis=1).astype(jnp.int32).astype(jnp.int16)
        ready[first : first + group] = coded
        copy = pltpu.make_async_copy(
            ready.at[pl.ds(first, group)],
            out.at[pl.ds(first, group)],
            sent.at[first // group],
        )
        copy.start()
        leaving.append(copy)
    for copy in leaving:
        copy.wait()


def routed_rows(
    counts, small, mid, grads, proj_small, proj_mid, owners, device_count, padded, group
):
    sources = (owners, small, proj_small, mid, proj_mid)
    block = (device_count, padded // 2 + padded // 3, LANES)
    held = [pltpu.VMEM(source.shape, source.dtype) for source in sources]
    for at in (3, 6):
        held.insert(at, pltpu.VMEM(grads.shape[1:], grads.dtype))

    def kernel(counts, owners, small, p_small, mid, p_mid, grads, *rest):
        sources = (owners, small, p_small, grads.at[0], mid, p_mid, grads.at[1])
        routing_kernel(device_count, padded, group, counts, *sources, *rest)

    return pl.pallas_call(
        kernel,
        out_shape=jax.ShapeDtypeStruct(block, jnp.int16),
        in_specs=[pl.BlockSpec(memory_space=pltpu.SMEM)]
        + [pl.BlockSpec(memory_space=pltpu.HBM)] * 6,
        out_specs=pl.BlockSpec(memory_space=pl.ANY),
        scratch_shapes=held
        + [
            pltpu.VMEM((5, grads.shape[1], 2 * LANES), jnp.bfloat16),
            pltpu.VMEM(block, jnp.int16),
            pltpu.SemaphoreType.DMA((7,)),
            pltpu.SemaphoreType.DMA((device_count // group,)),
        ],
        compiler_params=pltpu.CompilerParams(vmem_limit_bytes=56 * MIB),
        name="routed_rows",
    )(counts, *sources, grads)


def fetch_kernel(routed, out):
    out[...] = routed[...]


def fetched(routed):
    return pl.pallas_call(
        fetch_kernel,
        out_shape=jax.ShapeDtypeStruct(routed.shape, routed.dtype),
        compiler_params=pltpu.CompilerParams(vmem_limit_bytes=4 * MIB),
        name="fetched",
    )(routed)


def shares_kernel(pieces, routed, out):
    first = pieces.shape[1] - 3 * CHUNK
    summed = 0.0
    for device in range(pieces.shape[0]):
        summed = summed + share_values(pieces[device, first:].astype(jnp.float32))
    summed = jnp.where(share_row(summed.shape), 0.0, summed)
    exponent = code_exponent(jnp.broadcast_to(row_top(jnp.abs(summed)), summed.shape))
    coded = code(summed, exponent)
    coded = jnp.where(share_row(summed.shape), exponent_row(exponent), coded)
    coded = jnp.concatenate([coded[:, :LANES], coded[:, LANES:]], axis=0)
    coded = coded.astype(jnp.int32).astype(jnp.int16)
    share = 2 * CHUNK
    out[:, :share] = jnp.broadcast_to(coded[None], (out.shape[0],) + coded.shape)
    out[:, share:] = routed[...]


def with_shares(pieces, routed):
    device_count, rows, _ = routed.shape
    block = (device_count, 2 * CHUNK + rows, LANES)
    return pl.pallas_call(
        shares_kernel,
        out_shape=jax.ShapeDtypeStruct(block, routed.dtype),
        compiler_params=pltpu.CompilerParams(vmem_limit_bytes=8 * MIB),
        name="with_shares",
    )(pieces, routed)


def projecting_kernel(
    padded, everything, wide, rest, proj_small, proj_mid, proj_wide, out, weights
):
    group = rest.shape[0]
    w_small, w_mid, w_wide = proj_small.shape[0], proj_mid.shape[0], proj_wide.shape[0]
    out_width = proj_wide.shape[1]
    half, third = padded // 2, padded // 3
    share_end, mid_end, _ = packing(padded)

    @pl.when(pl.program_id(0) == 0)
    def _():
        shares = []
        for device in range(-(-(w_wide + w_mid + w_small) // (CHUNK - 1))):
            share = everything[device, 0:share_end, :].astype(jnp.float32)
            share = jnp.concatenate([share[:CHUNK], share[CHUNK:]], axis=1)
            scale = code_scale(exponent_column(share))
            shares.append((share * scale)[: CHUNK - 1])
        total = jnp.concatenate(shares, axis=0)
        tiers = (
            (proj_wide, 0, (0,)),
            (proj_mid, w_wide, (0, w_mid)),
            (proj_small, w_wide + w_mid, (0, w_small, 2 * w_small)),
        )
        index = 0
        for projection, start, places in tiers:
            part = total[start : start + projection.shape[0]]
            factor = STEP_NORM / jnp.sqrt(jnp.sum(part * part, keepdims=True) + 1e-06)
            fresh = projection[...] - factor * part
            for place in places:
                for piece in halves(widened(fresh, place)):
                    weights[index, 0:LANES] = piece * jnp.bfloat16(256.0)
                    weights[index, LANES:] = piece
                    index += 1

    def split_code(value):
        value = value.reshape(-1, LANES)
        upper = jnp.floor(value * (1.0 / 256.0))
        lower = value - 256.0 * upper
        return jnp.concatenate([upper, lower], axis=1).astype(jnp.bfloat16)

    def projected(left, index):
        product = contract(left, weights[2 * index], 1, 0)
        product = product + contract(left, weights[2 * index + 1], 1, 0)
        return product.reshape(group, -1, out_width)

    codes = rest[...].astype(jnp.float32)
    small_codes = codes[:, mid_end:]
    small_rows = split_code(small_codes)
    mid_rows = split_code(codes[:, share_end:mid_end])
    wide_codes = wide[...].astype(jnp.float32)
    wide_rows = split_code(wide_codes[:, 0:padded])
    row = lax.broadcasted_iota(jnp.int32, (group, padded, LANES), 1) + CHUNK
    lane = lax.broadcasted_iota(jnp.int32, (group, padded, LANES), 2)
    at = padded + CHUNK - 1
    scales = jnp.where(row == lane, wide_codes[:, at : at + 1], 0.0)
    wide_scale = code_scale(jnp.sum(scales, axis=2, keepdims=True))
    scales = code_scale(small_codes)
    spare = 3 * w_small
    slot_scales = [
        jnp.concatenate([scales[:, :, at : at + 1] for at in range(first, first + 3)], axis=1)
        for first in (spare, spare + 3)
    ]
    products = (
        ([projected(small_rows, 3 + at) for at in range(3)], slot_scales[0]),
        ([projected(mid_rows, 1 + at) for at in range(2)], slot_scales[1]),
        ([projected(wide_rows, 0)], wide_scale),
    )
    for tier, (parts, scale) in enumerate(products):
        product = jnp.concatenate(parts, axis=1) * scale
        product = product.astype(jnp.bfloat16).reshape(group * padded, out_width)
        out[:, tier * out_width : (tier + 1) * out_width] = product


def projected_rows(wide, rest, projections, padded, group):
    device_count = rest.shape[0]
    out_width = projections[2].shape[1]
    rows = group * padded
    return pl.pallas_call(
        functools.partial(projecting_kernel, padded),
        grid=(device_count // group,),
        out_shape=jax.ShapeDtypeStruct(
            (device_count * padded, 3 * out_width), jnp.bfloat16
        ),
        in_specs=[
            whole(rest.shape),
            pl.BlockSpec((group,) + wide.shape[1:], lambda step: (step, 0, 0)),
            pl.BlockSpec((group,) + rest.shape[1:], lambda step: (step, 0, 0)),
            *[whole(projection.shape) for projection in projections],
        ],
        out_specs=pl.BlockSpec((rows, 3 * out_width), lambda step: (step, 0)),
        scratch_shapes=[pltpu.VMEM((12, 2 * LANES, out_width), jnp.bfloat16)],
        compiler_params=pltpu.CompilerParams(vmem_limit_bytes=16 * MIB),
        name="projected_rows",
    )(rest, wide, rest, *projections)


def exchange(blocks):
    return lax.all_to_all(
        blocks, ("rows", "serve"), split_axis=0, concat_axis=0, tiled=True
    )


def local(
    rows_small, rows_mid, rows_wide, row_grads, proj_small, proj_mid, proj_wide, counts, owners
):
    device_count = lax.axis_size("rows") * lax.axis_size("serve")
    slots_here = rows_small.shape[0]
    capacity = max(2, slots_here // device_count + slots_here // (2 * device_count))
    padded = -(-capacity // 48) * 48
    out_width = row_grads.shape[2]
    group = 8 if device_count % 8 == 0 else 1
    small, mid = rows_small.T, rows_mid.T
    counts = counts.T
    owners = jnp.transpose(owners, (0, 2, 1))
    projections = (proj_small, proj_mid, proj_wide)
    sizes = (device_count, padded, 2 * group)
    first = first_blocks(
        counts, small, mid, rows_wide, row_grads, proj_wide, owners, *sizes
    )
    first = exchange(first)
    second = routed_rows(
        counts, small, mid, row_grads, proj_small, proj_mid, owners, *sizes
    )
    second = exchange(with_shares(first, fetched(second)))
    served = projected_rows(first, second, projections, padded, group)
    if padded != capacity:
        served = served.reshape(device_count, padded, 3 * out_width)[:, :capacity]
        served = served.reshape(device_count * capacity, 3 * out_width)
    return served


def solution(mesh):
    return jax.shard_map(
        local,
        mesh=mesh,
        in_specs=(
            P(("rows", "serve"), None),
            P(("rows", "serve"), None),
            P(("rows", "serve"), None),
            P(None, ("rows", "serve"), None),
            P(),
            P(),
            P(),
            P(None, ("rows", "serve")),
            P(None, ("rows", "serve"), None),
        ),
        out_specs=P(("rows", "serve"), None),
        check_vma=False,
    )
```
